256 devices in a mesh: seq: 16 (over y_hi, z), chan: 16 (over x, y_lo, core).
Axes of the slice: x: 4, y: 4 (y_hi: 2, y_lo: 2; y = y_hi * 2 + y_lo), z: 8, core: 2. Of those that a mesh axis runs over, the one named last changes fastest.
Arguments:
- query_act: bfloat16 [4096, 4096], P('chan', 'seq'), may hold values from -6 to 6
- key_act: bfloat16 [4096, 4096], P('chan', 'seq'), may hold values from -6 to 6
- value_act: bfloat16 [4096, 4096], P('chan', 'seq'), may hold values from -6 to 6
- filter_taps: float32 [4096, 4096], P('chan', 'seq'), may hold values from -0.09375 to 0.09375
- skip_gain: float32 [4096], P('chan'), may hold values from -4 to 4
- out_weight: bfloat16 [4096, 8192], P('chan'), may hold values from -0.125 to 0.125
Outputs:
- mixed: bfloat16 [8192, 4096], P('chan', 'seq')
The draws below stay inside these ranges and needn't reach their ends.
All inputs are finite; a program needn't handle non-finite values.
Results may differ from the reference program's by a relative error of at most 0.025.
Values may be sent and summed in bfloat16 or wider, within the bound.
No kernel may reach another device: no remote copies, remote signals or barrier semaphores. Data moves between devices by JAX's collectives and lax.ppermute only.
A program may use at most 64 MiB of HBM per device.

```python
import jax
import jax.numpy as jnp
from jax import lax

DM = 8192
CHG = 256
SEQ_LEN = 4096
CH = 4096
N_CHAN = 16


def spiked(drawn, stream_key, source, target, blocks, factor):
    def block_of(position):
        return (jnp.arange(drawn.shape[position]) // (drawn.shape[position] // blocks)).reshape((-1,) + (1,) * (drawn.ndim - 1 - position))

    first = jax.random.permutation(stream_key, blocks)[block_of(target)]
    far = (block_of(target) + blocks // 2) % blocks
    return jnp.where((block_of(source) == first) | (block_of(source) == far), factor * drawn, drawn)


def steps_of(own_key, shape, split, least, high):
    level, own = 1.0, jax.random.fold_in(own_key, 6)
    for dim, parts in split:
        steps = jnp.exp(jax.random.uniform(jax.random.fold_in(own, dim), (parts,), jnp.float32, least / len(split), high / len(split)))
        level = level * jnp.repeat(steps, shape[dim] // parts).reshape([-1 if axis == dim else 1 for axis in range(len(shape))])
    return level


def noise(rng, extent, width, bound, shards=(), dtype=jnp.bfloat16):
    values = width * jax.random.normal(rng, extent, jnp.float32)
    if shards:
        values = values * steps_of(rng, extent, shards, -0.22, 0.18)
    return jnp.clip(values, -bound, bound).astype(dtype)


def bell_draw_with(own_key, shape, scale, bound, pieces, heavy, kind=jnp.bfloat16):
    array = scale * jax.random.normal(own_key, shape, jnp.float32)
    if pieces:
        array = array * steps_of(own_key, shape, pieces, -0.22, 0.18)
    return jnp.clip(spiked(array, jax.random.fold_in(own_key, 3), *heavy), -bound, bound).astype(kind)


def setup_inputs(seed: int = 0) -> dict:
    keys = jax.random.split(jax.random.key(seed), 7)
    query_act = noise(keys[0], (CH, SEQ_LEN), 1.0, 6.0, ((0, 16), (1, 16)))
    key_act = noise(keys[1], (CH, SEQ_LEN), 1.0, 6.0, ((0, 16), (1, 16)))
    value_act = noise(keys[2], (CH, SEQ_LEN), 1.0, 6.0, ((0, 16), (1, 16)))
    filter_taps = noise(keys[3], (CH, SEQ_LEN), SEQ_LEN ** -0.5, 0.09375, ((0, 16), (1, 16)), jnp.float32)
    skip_gain = noise(keys[4], (CH,), 1.0, 4.0, ((0, 16),), jnp.float32)
    out_weight = bell_draw_with(keys[5], (CH, DM), CH ** -0.5, 0.125, ((0, 16),), (0, 1, 16, 2.0))
    return {"query_act": query_act, "key_act": key_act, "value_act": value_act, "filter_taps": filter_taps, "skip_gain": skip_gain, "out_weight": out_weight}


def reference(query_act, key_act, value_act, filter_taps, skip_gain, out_weight):
    gated_input = key_act.astype(jnp.float32) * value_act.astype(jnp.float32)
    padded_len = 2 * SEQ_LEN
    input_freq = jnp.fft.rfft(gated_input, n=padded_len, axis=1)
    filter_freq = jnp.fft.rfft(filter_taps, n=padded_len, axis=1)
    long_conv = jnp.fft.irfft(input_freq * filter_freq, n=padded_len, axis=1)[:, :SEQ_LEN]
    gated_rows = (query_act.astype(jnp.float32) * (long_conv + skip_gain[:, None] * gated_input)).astype(jnp.bfloat16)
    group_rows = gated_rows.reshape(N_CHAN, CHG, SEQ_LEN)
    group_weights = out_weight.reshape(N_CHAN, CHG, DM)

    def add_group(summed, pair_data):
        rows_part, weight_part = pair_data
        group_part = lax.dot_general(weight_part, rows_part, (((0,), (0,)), ((), ())), preferred_element_type=jnp.float32)
        rounded = lax.optimization_barrier(group_part.astype(jnp.bfloat16))
        return summed + rounded.astype(jnp.float32), None

    summed, unused = lax.scan(add_group, jnp.zeros((DM, SEQ_LEN), jnp.float32), (group_rows, group_weights))
    return summed.astype(jnp.bfloat16)
```

```python
import functools

import jax
import jax.numpy as jnp
from jax import lax
from jax.experimental import pallas as pl
from jax.experimental.pallas import tpu as pltpu
from jax.sharding import PartitionSpec as P

N_SEQ, N_X, N_CHAN = 16, 4, 16
LANES = 128
VMEM = pl.BlockSpec(memory_space=pltpu.VMEM)


def chan_perm(dx, dy, dk):
    return [
        ((x * 2 + y) * 2 + k, ((x + dx) % N_X * 2 + (y ^ dy)) * 2 + (k ^ dk))
        for x in range(N_X)
        for y in range(2)
        for k in range(2)
    ]


def ring_y_perm(step, dk):
    pairs = []
    for y in range(4):
        to = (y + step) % 4
        for z in range(8):
            for x in range(N_X):
                for k in range(2):
                    source = (y // 2 * 8 + z) * N_CHAN + (x * 2 + y % 2) * 2 + k
                    target = (to // 2 * 8 + z) * N_CHAN + (x * 2 + to % 2) * 2 + (k ^ dk)
                    pairs.append((source, target))
    return pairs


def pack_kernel(key_ref, value_ref, taps_ref, out_ref):
    for dst in range(N_SEQ):
        rows = slice(16 * dst, 16 * dst + 16)
        for half in range(2):
            cols = slice(LANES * half, LANES * half + LANES)
            gated = key_ref[rows, cols].astype(jnp.float32) * value_ref[rows, cols].astype(jnp.float32)
            out_ref[dst, 0, half] = gated.astype(jnp.bfloat16)
            out_ref[dst, 1, half] = taps_ref[rows, cols].astype(jnp.bfloat16)


def conv_kernel(recv_ref, out_ref, xs, hs, ys, xpad, lhs, rhs):
    for s in range(N_SEQ):
        for half in range(2):
            a = 2 * s + half
            xs[16 * a : 16 * a + 16, :] = recv_ref[s, 0, half].astype(jnp.float32)
            hs[16 * a : 16 * a + 16, :] = recv_ref[s, 1, half].astype(jnp.float32)
    for b in range(2):
        xpad[b, 0:32, :] = jnp.zeros((32, LANES), jnp.float32)
    lane = lax.broadcasted_iota(jnp.int32, (8, LANES), 1)
    row = lax.broadcasted_iota(jnp.int32, (8, LANES), 0)

    def one(c, b):
        xpad[b, 32:64, :] = xs[pl.ds(c, 32, stride=16), :]
        for d in range(32):
            lhs[b, :, LANES * d : LANES * d + LANES] = xpad[b, 32 - d : 64 - d, :].astype(jnp.bfloat16)
        before = [jnp.zeros((8, LANES), jnp.float32)] * 16
        for i in range(32):
            taps = jnp.broadcast_to(hs[pl.ds(16 * i + c, 1), :], (8, LANES))
            turned = [pltpu.roll(taps, 8 * g, 1, stride=1, stride_axis=0) for g in range(16)]
            tiles = [jnp.where(lane >= row + 8 * g, turned[g], before[g]) for g in range(16)]
            for g in range(0, 16, 2):
                pair = jnp.concatenate([tiles[g], tiles[g + 1]], 0).astype(jnp.bfloat16)
                rhs[b, LANES * i + 8 * g : LANES * i + 8 * g + 16, :] = pair
            before = turned
        ys[pl.ds(c, 32, stride=16), :] = jnp.dot(lhs[b], rhs[b], preferred_element_type=jnp.float32)

    def body(p, carry):
        one(2 * p, 0)
        one(2 * p + 1, 1)
        return carry

    lax.fori_loop(0, 8, body, 0)
    for s in range(N_SEQ):
        for half in range(2):
            a = 2 * s + half
            out_ref[s, half] = ys[16 * a : 16 * a + 16, :].astype(jnp.bfloat16)


def rows_kernel(query_ref, key_ref, value_ref, gain_ref, conv_ref, out_ref):
    for src in range(N_SEQ):
        rows = slice(16 * src, 16 * src + 16)
        gain = gain_ref[rows, :]
        for half in range(2):
            cols = slice(LANES * half, LANES * half + LANES)
            gated = key_ref[rows, cols].astype(jnp.float32) * value_ref[rows, cols].astype(jnp.float32)
            total = conv_ref[src, half].astype(jnp.float32) + gain * gated
            out_ref[rows, cols] = (query_ref[rows, cols].astype(jnp.float32) * total).astype(jnp.bfloat16)


def slice_kernel(place_ref, own, core, ring, diag, own_out, core_out, ring_a, ring_b, diag_a, diag_b):
    own_out[0] = own[...]
    core_out[0] = core[...]
    ring_a[0] = ring[:128, :]
    ring_b[0] = ring[128:, :]
    diag_a[0] = diag[:128, :]
    diag_b[0] = diag[128:, :]


def weight_slices(weight, place):
    def column(dy, dk):
        def index(n, place):
            return (0, ((place[0] + n) % N_X * 2 + (place[1] ^ dy)) * 2 + (place[2] ^ dk))

        return pl.BlockSpec((256, 512), index)

    whole = pl.BlockSpec((1, 256, 512), lambda n, place: (n, 0, 0))
    part = pl.BlockSpec((1, 128, 512), lambda n, place: (n, 0, 0))
    return pl.pallas_call(
        slice_kernel,
        grid_spec=pltpu.PrefetchScalarGridSpec(
            num_scalar_prefetch=1,
            grid=(N_X,),
            in_specs=[column(0, 0), column(0, 1), column(1, 0), column(1, 1)],
            out_specs=[whole, whole, part, part, part, part],
        ),
        out_shape=[jax.ShapeDtypeStruct((N_X, 256, 512), jnp.bfloat16)] * 2
        + [jax.ShapeDtypeStruct((N_X, 128, 512), jnp.bfloat16)] * 4,
        cost_estimate=pl.CostEstimate(flops=0, bytes_accessed=8 * 2**20, transcendentals=0),
        compiler_params=pltpu.CompilerParams(vmem_limit_bytes=16 * 2**20),
        name="weight_slices",
    )(place, weight, weight, weight, weight)


def project_kernel(own_w, core_w, ring_a, ring_b, diag_a, diag_b, own_r, core_r, ring_r, diag_r, out_ref):
    def term(weight, rows):
        return lax.dot_general(weight, rows, (((0,), (0,)), ((), ())), preferred_element_type=jnp.float32)

    total = term(own_w[0], own_r[...])
    total += term(core_w[0], core_r[...])
    total += term(ring_a[0], ring_r[:128, :])
    total += term(ring_b[0], ring_r[128:, :])
    total += term(diag_a[0], diag_r[:128, :])
    total += term(diag_b[0], diag_r[128:, :])
    out_ref[...] = total.astype(out_ref.dtype)


def project(n, weights, rows, dtype):
    whole = pl.BlockSpec((1, 256, 512), lambda i: (n, 0, 0))
    part = pl.BlockSpec((1, 128, 512), lambda i: (n, 0, 0))
    full = pl.BlockSpec((256, 256), lambda i: (0, 0))
    return pl.pallas_call(
        project_kernel,
        grid=(1,),
        out_shape=jax.ShapeDtypeStruct((512, 256), dtype),
        in_specs=[whole, whole, part, part, part, part, full, full, full, full],
        out_specs=pl.BlockSpec((512, 256), lambda i: (0, 0)),
        cost_estimate=pl.CostEstimate(flops=2 * 1024 * 512 * 256, bytes_accessed=2 * 2**20, transcendentals=0),
        compiler_params=pltpu.CompilerParams(vmem_limit_bytes=16 * 2**20),
        name="project",
    )(*weights, *rows)


def local(query_act, key_act, value_act, filter_taps, skip_gain, out_weight):
    chan = lax.axis_index("chan")
    send = pl.pallas_call(
        pack_kernel,
        out_shape=jax.ShapeDtypeStruct((N_SEQ, 2, 2, 16, LANES), jnp.bfloat16),
        in_specs=[VMEM] * 3,
        out_specs=VMEM,
        name="pack",
    )(key_act, value_act, filter_taps)
    place = jnp.stack([chan // 4, chan // 2 % 2, chan % 2]).astype(jnp.int32)
    own_w, core_w, ring_a, ring_b, diag_a, diag_b = weight_slices(out_weight, place)
    both = ("seq", "chan")
    core_w = lax.ppermute(core_w, "chan", chan_perm(0, 0, 1))
    ring_a = lax.ppermute(ring_a, both, ring_y_perm(1, 0))
    ring_b = lax.ppermute(ring_b, both, ring_y_perm(-1, 0))
    diag_a = lax.ppermute(diag_a, both, ring_y_perm(1, 1))
    diag_b = lax.ppermute(diag_b, both, ring_y_perm(-1, 1))
    weights = (own_w, core_w, ring_a, ring_b, diag_a, diag_b)

    recv = lax.all_to_all(send, "seq", 0, 0, tiled=True)
    conv = pl.pallas_call(
        conv_kernel,
        out_shape=jax.ShapeDtypeStruct((N_SEQ, 2, 16, LANES), jnp.bfloat16),
        in_specs=[VMEM],
        out_specs=VMEM,
        scratch_shapes=[pltpu.VMEM((512, LANES), jnp.float32)] * 3
        + [
            pltpu.VMEM((2, 64, LANES), jnp.float32),
            pltpu.VMEM((2, 32, 4096), jnp.bfloat16),
            pltpu.VMEM((2, 4096, LANES), jnp.bfloat16),
        ],
        cost_estimate=pl.CostEstimate(flops=2 * 16 * 4096 * 4096, bytes_accessed=2**20, transcendentals=0),
        compiler_params=pltpu.CompilerParams(vmem_limit_bytes=32 * 2**20),
        name="conv",
    )(recv)
    conv = lax.all_to_all(conv, "seq", 0, 0, tiled=True)
    own_r = pl.pallas_call(
        rows_kernel,
        out_shape=jax.ShapeDtypeStruct((256, 256), jnp.bfloat16),
        in_specs=[VMEM] * 5,
        out_specs=VMEM,
        name="rows",
    )(query_act, key_act, value_act, skip_gain[:, None], conv)
    core_r = lax.ppermute(own_r, "chan", chan_perm(0, 0, 1))
    ring_r = lax.ppermute(own_r, "chan", chan_perm(0, 1, 0))
    diag_r = lax.ppermute(ring_r, "chan", chan_perm(0, 0, 1))
    rows = (own_r, core_r, ring_r, diag_r)
    far = lax.ppermute(project(2, weights, rows, jnp.bfloat16), "chan", chan_perm(2, 0, 0))
    up = lax.ppermute(project(1, weights, rows, jnp.bfloat16), "chan", chan_perm(1, 0, 0))
    down = lax.ppermute(project(3, weights, rows, jnp.bfloat16), "chan", chan_perm(-1, 0, 0))
    own = project(0, weights, rows, jnp.float32)
    total = own + far.astype(jnp.float32) + up.astype(jnp.float32) + down.astype(jnp.float32)
    return total.astype(jnp.bfloat16)


def solution(mesh):
    placed = (
        P("chan", "seq"),
        P("chan", "seq"),
        P("chan", "seq"),
        P("chan", "seq"),
        P("chan"),
        P("chan", None),
    )
    return jax.shard_map(
        local, mesh=mesh, in_specs=placed, out_specs=P("chan", "seq"), check_vma=False
    )
```

```python
import functools

import jax
import jax.numpy as jnp
from jax import lax
from jax.experimental import pallas as pl
from jax.experimental.pallas import tpu as pltpu
from jax.sharding import PartitionSpec as P

N_SEQ, N_X, N_CHAN = 16, 4, 16
LANES = 128
VMEM = pl.BlockSpec(memory_space=pltpu.VMEM)
SMEM = pl.BlockSpec(memory_space=pltpu.SMEM)
ANY = pl.BlockSpec(memory_space=pl.ANY)


def chan_perm(dx, dy, dk):
    return [
        ((x * 2 + y) * 2 + k, ((x + dx) % N_X * 2 + (y ^ dy)) * 2 + (k ^ dk))
        for x in range(N_X)
        for y in range(2)
        for k in range(2)
    ]


def ring_y_perm(step, dk):
    pairs = []
    for y in range(4):
        to = (y + step) % 4
        for z in range(8):
            for x in range(N_X):
                for k in range(2):
                    source = (y // 2 * 8 + z) * N_CHAN + (x * 2 + y % 2) * 2 + k
                    target = (to // 2 * 8 + z) * N_CHAN + (x * 2 + to % 2) * 2 + (k ^ dk)
                    pairs.append((source, target))
    return pairs


def seq_y_groups():
    return [
        [seq * N_CHAN + (x * 2 + y) * 2 + k for seq in range(N_SEQ) for y in range(2)]
        for x in range(N_X)
        for k in range(2)
    ]


def pack_kernel(query_ref, key_ref, value_ref, taps_ref, out_ref):
    for dst in range(N_SEQ):
        rows = slice(16 * dst, 16 * dst + 16)
        for half in range(2):
            cols = slice(LANES * half, LANES * half + LANES)
            gated = key_ref[rows, cols].astype(jnp.float32) * value_ref[rows, cols].astype(jnp.float32)
            out_ref[dst, 0, half] = gated.astype(jnp.bfloat16)
            out_ref[dst, 1, half] = taps_ref[rows, cols].astype(jnp.bfloat16)
            out_ref[dst, 2, half] = query_ref[rows, cols]


def conv_kernel(recv_ref, gain_ref, out_ref, xs, hs, ys, xpad, done, sems):
    for s in range(N_SEQ):
        for half in range(2):
            rows = slice(32 * s + 16 * half, 32 * s + 16 * half + 16)
            xs[rows, :] = recv_ref[s, 0, half].astype(jnp.float32)
            hs[rows, :] = recv_ref[s, 1, half].astype(jnp.float32)
    for b in range(2):
        xpad[b, 0:32, :] = jnp.zeros((32, LANES), jnp.float32)
    lane = lax.broadcasted_iota(jnp.int32, (8, LANES), 1)
    row = lax.broadcasted_iota(jnp.int32, (8, LANES), 0)
    inside = [lane + row < LANES - 8 * g for g in range(16)]

    def body(p, carry):
        for b in range(2):
            xpad[b, 32:64, :] = xs[pl.ds(2 * p + b, 32, stride=16), :]
        before = [jnp.zeros((8, LANES), jnp.float32)] * 2
        total = jnp.zeros((64, 2 * LANES), jnp.float32)
        for d in range(32):
            shifted = jnp.concatenate([xpad[b, 32 - d : 64 - d, :] for b in range(2)], 0).astype(jnp.bfloat16)
            blocks = []
            for b in range(2):
                taps = jnp.broadcast_to(hs[pl.ds(16 * d + 2 * p + b, 1), :], (8, LANES))
                tiles = [
                    pltpu.roll(jnp.where(inside[g], taps, before[b]), 8 * g, 1, stride=1, stride_axis=0)
                    for g in range(16)
                ]
                before[b] = taps
                blocks.append(jnp.concatenate(tiles, 0).astype(jnp.bfloat16))
            total += jnp.dot(shifted, jnp.concatenate(blocks, 1), preferred_element_type=jnp.float32)
        ys[pl.ds(2 * p, 32, stride=16), :] = total[:32, :LANES]
        ys[pl.ds(2 * p + 1, 32, stride=16), :] = total[32:, LANES:]
        return carry

    lax.fori_loop(0, 8, body, 0, unroll=2)
    for s in range(N_SEQ):
        for half in range(2):
            rows = slice(32 * s + 16 * half, 32 * s + 16 * half + 16)
            total = ys[rows, :] + gain_ref[...] * xs[rows, :]
            done[s, half] = (recv_ref[s, 2, half].astype(jnp.float32) * total).astype(jnp.bfloat16)
    copies = [pltpu.make_async_copy(done, out_ref.at[:, y], sems.at[y]) for y in range(2)]
    for copy in copies:
        copy.start()
    for copy in copies:
        copy.wait()


def slice_kernel(parts, place_ref, *refs):
    outs, sems = refs[-len(parts) - 1 : -1], refs[-1]
    copies = []
    for number, (other, out) in enumerate(zip(parts, outs)):
        for n in range(N_X):
            column = (place_ref[0] // 4 + n) % N_X * 4 + ((place_ref[0] % 4) ^ other)
            source = refs[0].at[:, pl.ds(pl.multiple_of(column * 512, 512), 512)]
            copies.append(pltpu.make_async_copy(source, out.at[n], sems.at[number, n]))
            copies[-1].start()
    for copy in copies:
        copy.wait()


def weight_slices(parts, weight, place, *after):
    return pl.pallas_call(
        functools.partial(slice_kernel, parts),
        in_specs=[SMEM] + [ANY] * (1 + len(after)),
        out_specs=[VMEM] * len(parts),
        out_shape=[jax.ShapeDtypeStruct((N_X, 256, 512), jnp.bfloat16)] * len(parts),
        scratch_shapes=[pltpu.SemaphoreType.DMA((len(parts), N_X))],
        cost_estimate=pl.CostEstimate(flops=0, bytes_accessed=len(parts) * 2**20, transcendentals=0),
        compiler_params=pltpu.CompilerParams(vmem_limit_bytes=8 * 2**20),
        name="weight_slices",
    )(place, weight, *after)


def by_position(rows_ref, y):
    halves = [jnp.concatenate([rows_ref[src, y, half] for src in range(N_SEQ)], 0) for half in range(2)]
    return jnp.concatenate([half.astype(jnp.float32).T.astype(jnp.bfloat16) for half in halves], 0)


def mine_kernel(place_ref, own_w, ring_w, rows_ref, *outs):
    y = place_ref[0] // 2 % 2
    own, ring = by_position(rows_ref, y), by_position(rows_ref, 1 - y)
    for n in range(N_X):
        total = jnp.dot(own, own_w[n], preferred_element_type=jnp.float32)
        outs[n][...] = total + jnp.dot(ring, ring_w[n], preferred_element_type=jnp.float32)


def mine_terms(place, own_w, ring_w, rows):
    return pl.pallas_call(
        mine_kernel,
        out_shape=[jax.ShapeDtypeStruct((256, 512), jnp.float32)] * N_X,
        in_specs=[SMEM] + [VMEM] * 3,
        out_specs=[VMEM] * N_X,
        cost_estimate=pl.CostEstimate(flops=2 * 512 * 2048 * 256, bytes_accessed=2**20, transcendentals=0),
        compiler_params=pltpu.CompilerParams(vmem_limit_bytes=12 * 2**20),
        name="mine_terms",
    )(place, own_w, ring_w, rows)


def far_kernel(place_ref, mine, core_w, diag_w, rows_ref, out_ref, core_ref):
    y = place_ref[0] // 2 % 2
    core_ref[:, :256] = by_position(rows_ref, y)
    core_ref[:, 256:] = by_position(rows_ref, 1 - y)
    core_kernel(2, mine, core_w, diag_w, core_ref, None, out_ref)


def far_term(place, mine, core_w, diag_w, rows):
    return pl.pallas_call(
        far_kernel,
        out_shape=[jax.ShapeDtypeStruct((256, 512), jnp.bfloat16)] * 2,
        in_specs=[SMEM] + [VMEM] * 4,
        out_specs=[VMEM] * 2,
        cost_estimate=pl.CostEstimate(flops=2 * 512 * 512 * 256, bytes_accessed=2**20, transcendentals=0),
        compiler_params=pltpu.CompilerParams(vmem_limit_bytes=8 * 2**20),
        name="far_term",
    )(place, mine, core_w, diag_w, rows)


def core_kernel(n, mine, core_w, diag_w, core_r, after, out_ref):
    total = mine[...] + jnp.dot(core_r[:, :256], core_w[n], preferred_element_type=jnp.float32)
    total += jnp.dot(core_r[:, 256:], diag_w[n], preferred_element_type=jnp.float32)
    out_ref[...] = total.astype(out_ref.dtype)


def add_core(n, mine, core_w, diag_w, core_r, after, dtype):
    return pl.pallas_call(
        functools.partial(core_kernel, n),
        out_shape=jax.ShapeDtypeStruct((256, 512), dtype),
        in_specs=[VMEM] * 4 + [ANY],
        out_specs=VMEM,
        cost_estimate=pl.CostEstimate(flops=2 * 512 * 512 * 256, bytes_accessed=2**20, transcendentals=0),
        compiler_params=pltpu.CompilerParams(vmem_limit_bytes=8 * 2**20),
        name="add_core",
    )(mine, core_w, diag_w, core_r, after)


def two_kernel(own, far, out_ref):
    out_ref[...] = own[...] + far[...].astype(jnp.float32)


def sum_kernel(two, up, down, out_ref):
    total = two[...] + up[...].astype(jnp.float32) + down[...].astype(jnp.float32)
    out_ref[...] = total.T.astype(jnp.bfloat16)


def local(query_act, key_act, value_act, filter_taps, skip_gain, out_weight):
    chan = lax.axis_index("chan")
    both = ("seq", "chan")
    send = pl.pallas_call(
        pack_kernel,
        out_shape=jax.ShapeDtypeStruct((N_SEQ, 3, 2, 16, LANES), jnp.bfloat16),
        in_specs=[VMEM] * 4,
        out_specs=VMEM,
        name="pack",
    )(query_act, key_act, value_act, filter_taps)
    place = jnp.reshape(chan, (1,)).astype(jnp.int32)
    own_w, core_w, ring_w, diag_w = weight_slices((0, 1, 2, 3), out_weight, place, send)
    ring_w = lax.ppermute(ring_w, both, ring_y_perm(1, 0))
    diag_w = lax.ppermute(diag_w, both, ring_y_perm(-1, 1))
    core_w = lax.ppermute(core_w, "chan", chan_perm(0, 0, 1))

    gain = lax.dynamic_slice(skip_gain, (16 * lax.axis_index("seq"),), (16,))
    gain = jnp.broadcast_to(gain[:, None], (16, LANES))
    recv = lax.all_to_all(send, "seq", 0, 0, tiled=True)
    rows = pl.pallas_call(
        conv_kernel,
        out_shape=jax.ShapeDtypeStruct((N_SEQ, 2, 2, 16, LANES), jnp.bfloat16),
        in_specs=[VMEM, VMEM],
        out_specs=ANY,
        scratch_shapes=[pltpu.VMEM((512, LANES), jnp.float32)] * 3
        + [
            pltpu.VMEM((2, 64, LANES), jnp.float32),
            pltpu.VMEM((N_SEQ, 2, 16, LANES), jnp.bfloat16),
            pltpu.SemaphoreType.DMA((2,)),
        ],
        cost_estimate=pl.CostEstimate(flops=2 * 16 * 4096 * 4096, bytes_accessed=0, transcendentals=0),
        compiler_params=pltpu.CompilerParams(vmem_limit_bytes=8 * 2**20),
        name="conv",
    )(recv, gain)
    rows = jnp.reshape(rows, (2 * N_SEQ, 2, 16, LANES))
    rows = lax.all_to_all(rows, both, 0, 0, axis_index_groups=seq_y_groups(), tiled=True)
    rows = jnp.reshape(rows, (N_SEQ, 2, 2, 16, LANES))
    core_rows = lax.ppermute(rows, "chan", chan_perm(0, 0, 1))
    terms = mine_terms(place, own_w, ring_w, rows)
    far, core_r = far_term(place, terms[2], core_w, diag_w, core_rows)
    more = (core_w, diag_w, core_r)
    up = add_core(1, terms[1], *more, far, jnp.bfloat16)
    down = add_core(3, terms[3], *more, up, jnp.bfloat16)
    own = add_core(0, terms[0], *more, down, jnp.float32)
    far = lax.ppermute(far, "chan", chan_perm(2, 0, 0))
    up = lax.ppermute(up, "chan", chan_perm(1, 0, 0))
    down = lax.ppermute(down, "chan", chan_perm(-1, 0, 0))
    two = pl.pallas_call(
        two_kernel,
        out_shape=jax.ShapeDtypeStruct((256, 512), jnp.float32),
        in_specs=[VMEM] * 2,
        out_specs=VMEM,
        compiler_params=pltpu.CompilerParams(vmem_limit_bytes=4 * 2**20),
        name="two",
    )(own, far)
    return pl.pallas_call(
        sum_kernel,
        out_shape=jax.ShapeDtypeStruct((512, 256), jnp.bfloat16),
        in_specs=[VMEM] * 3,
        out_specs=VMEM,
        compiler_params=pltpu.CompilerParams(vmem_limit_bytes=4 * 2**20),
        name="sum",
    )(two, up, down)


def solution(mesh):
    placed = (
        P("chan", "seq"),
        P("chan", "seq"),
        P("chan", "seq"),
        P("chan", "seq"),
        P("chan"),
        P("chan", None),
    )
    return jax.shard_map(
        local, mesh=mesh, in_specs=placed, out_specs=P("chan", "seq"), check_vma=False
    )
```

```python
import functools

import jax
import jax.numpy as jnp
from jax import lax
from jax.experimental import pallas as pl
from jax.experimental.pallas import tpu as pltpu
from jax.sharding import PartitionSpec as P

N_SEQ, N_X, N_CHAN = 16, 4, 16
LANES = 128
VMEM = pl.BlockSpec(memory_space=pltpu.VMEM)
SMEM = pl.BlockSpec(memory_space=pltpu.SMEM)
ANY = pl.BlockSpec(memory_space=pl.ANY)


def chan_perm(dx, dy, dk):
    return [
        ((x * 2 + y) * 2 + k, ((x + dx) % N_X * 2 + (y ^ dy)) * 2 + (k ^ dk))
        for x in range(N_X)
        for y in range(2)
        for k in range(2)
    ]


def ring_y_perm(step, dk):
    pairs = []
    for y in range(4):
        to = (y + step) % 4
        for z in range(8):
            for x in range(N_X):
                for k in range(2):
                    source = (y // 2 * 8 + z) * N_CHAN + (x * 2 + y % 2) * 2 + k
                    target = (to // 2 * 8 + z) * N_CHAN + (x * 2 + to % 2) * 2 + (k ^ dk)
                    pairs.append((source, target))
    return pairs


def seq_y_groups():
    return [
        [seq * N_CHAN + (x * 2 + y) * 2 + k for seq in range(N_SEQ) for y in range(2)]
        for x in range(N_X)
        for k in range(2)
    ]


def pack_kernel(query_ref, key_ref, value_ref, taps_ref, out_ref, token_ref):
    for dst in range(N_SEQ):
        rows = slice(16 * dst, 16 * dst + 16)
        for half in range(2):
            cols = slice(LANES * half, LANES * half + LANES)
            gated = key_ref[rows, cols].astype(jnp.float32) * value_ref[rows, cols].astype(jnp.float32)
            out_ref[dst, 0, half] = gated.astype(jnp.bfloat16)
            out_ref[dst, 1, half] = taps_ref[rows, cols].astype(jnp.bfloat16)
            out_ref[dst, 2, half] = query_ref[rows, cols]
    token_ref[...] = jnp.zeros_like(token_ref)


def conv_kernel(recv_ref, gain_ref, out_ref, xs, hs, ys, xpad, done, sems):
    for s in range(N_SEQ):
        for half in range(2):
            rows = slice(32 * s + 16 * half, 32 * s + 16 * half + 16)
            xs[rows, :] = recv_ref[s, 0, half].astype(jnp.float32)
            hs[rows, :] = recv_ref[s, 1, half].astype(jnp.float32)
    for b in range(2):
        xpad[b, 0:32, :] = jnp.zeros((32, LANES), jnp.float32)
    lane = lax.broadcasted_iota(jnp.int32, (8, LANES), 1)
    row = lax.broadcasted_iota(jnp.int32, (8, LANES), 0)
    inside = [lane + row < LANES - 8 * g for g in range(16)]

    def body(p, carry):
        for b in range(2):
            xpad[b, 32:64, :] = xs[pl.ds(2 * p + b, 32, stride=16), :]
        before = [jnp.zeros((8, LANES), jnp.float32)] * 2
        total = jnp.zeros((64, 2 * LANES), jnp.float32)
        for d in range(32):
            shifted = jnp.concatenate([xpad[b, 32 - d : 64 - d, :] for b in range(2)], 0).astype(jnp.bfloat16)
            blocks = []
            for b in range(2):
                taps = jnp.broadcast_to(hs[pl.ds(16 * d + 2 * p + b, 1), :], (8, LANES))
                tiles = [
                    pltpu.roll(jnp.where(inside[g], taps, before[b]), 8 * g, 1, stride=1, stride_axis=0)
                    for g in range(16)
                ]
                before[b] = taps
                blocks.append(jnp.concatenate(tiles, 0).astype(jnp.bfloat16))
            total += jnp.dot(shifted, jnp.concatenate(blocks, 1), preferred_element_type=jnp.float32)
        ys[pl.ds(2 * p, 32, stride=16), :] = total[:32, :LANES]
        ys[pl.ds(2 * p + 1, 32, stride=16), :] = total[32:, LANES:]
        return carry

    lax.fori_loop(0, 8, body, 0, unroll=8)
    for s in range(N_SEQ):
        for half in range(2):
            rows = slice(32 * s + 16 * half, 32 * s + 16 * half + 16)
            total = ys[rows, :] + gain_ref[...] * xs[rows, :]
            done[s, half] = (recv_ref[s, 2, half].astype(jnp.float32) * total).astype(jnp.bfloat16)
    copies = [pltpu.make_async_copy(done, out_ref.at[:, y], sems.at[y]) for y in range(2)]
    for copy in copies:
        copy.start()
    for copy in copies:
        copy.wait()


def slice_kernel(parts, place_ref, after_ref, weight_ref, *refs):
    outs, held, in_sems, out_sems = refs[: len(parts)], refs[len(parts) : -2], refs[-2], refs[-1]
    loads, stores = [], []
    for number, (other, steps) in enumerate(parts):
        for slot, n in enumerate(steps):
            column = (place_ref[0] // 4 + n) % N_X * 4 + ((place_ref[0] % 4) ^ other)
            source = weight_ref.at[:, pl.ds(pl.multiple_of(column * 512, 512), 512)]
            loads.append((number, pltpu.make_async_copy(source, held[number].at[slot], in_sems.at[number, slot])))
            loads[-1][1].start()
    for number in range(len(parts)):
        for at, load in loads:
            if at == number:
                load.wait()
        stores.append(pltpu.make_async_copy(held[number], outs[number], out_sems.at[number]))
        stores[-1].start()
    for store in stores:
        store.wait()


def weight_slices(parts, limit, weight, place, after):
    shapes = [(len(steps), 256, 512) for other, steps in parts]
    return pl.pallas_call(
        functools.partial(slice_kernel, parts),
        in_specs=[SMEM, ANY, ANY],
        out_specs=[ANY] * len(parts),
        out_shape=[jax.ShapeDtypeStruct(shape, jnp.bfloat16) for shape in shapes],
        scratch_shapes=[pltpu.VMEM(shape, jnp.bfloat16) for shape in shapes]
        + [pltpu.SemaphoreType.DMA((len(parts), N_X)), pltpu.SemaphoreType.DMA((len(parts),))],
        cost_estimate=pl.CostEstimate(flops=0, bytes_accessed=len(parts) * 2**20, transcendentals=0),
        compiler_params=pltpu.CompilerParams(vmem_limit_bytes=limit * 2**20),
        name="weight_slices",
    )(place, after, weight)


def by_position(rows_ref, y):
    halves = [jnp.concatenate([rows_ref[src, y, half] for src in range(N_SEQ)], 0) for half in range(2)]
    return jnp.concatenate([half.astype(jnp.float32).T.astype(jnp.bfloat16) for half in halves], 0)


def product(rows, first, second):
    total = jnp.dot(rows[:, :256], first, preferred_element_type=jnp.float32)
    return total + jnp.dot(rows[:, 256:], second, preferred_element_type=jnp.float32)


def mine_kernel(place_ref, own_w, ring_w, rows_ref, rows_out, out_ref):
    y = place_ref[0] // 2 % 2
    rows_out[:, :256] = by_position(rows_ref, y)
    rows_out[:, 256:] = by_position(rows_ref, 1 - y)
    out_ref[...] = product(rows_out, own_w[...], ring_w[2])


def far_kernel(place_ref, mine, core_w, diag_w, rows_ref, rows_out, out_ref):
    y = place_ref[0] // 2 % 2
    rows_out[:, :256] = by_position(rows_ref, y)
    rows_out[:, 256:] = by_position(rows_ref, 1 - y)
    out_ref[...] = (mine[...] + product(rows_out, core_w[2], diag_w[2])).astype(jnp.bfloat16)


def near_kernel(n, own_w, ring_w, core_w, diag_w, mine_r, core_r, after, out_ref):
    total = product(mine_r, own_w[...], ring_w[n]) + product(core_r, core_w[n], diag_w[n])
    out_ref[...] = total.astype(out_ref.dtype)


def two_kernel(own, far, out_ref):
    out_ref[...] = own[...] + far[...].astype(jnp.float32)


def sum_kernel(two, up, down, out_ref):
    total = two[...] + up[...].astype(jnp.float32) + down[...].astype(jnp.float32)
    out_ref[...] = total.T.astype(jnp.bfloat16)


def gain_kernel(gain_ref, after, out_ref):
    out_ref[...] = gain_ref[...]


def in_vmem(kernel, in_specs, outs, name, flops):
    return pl.pallas_call(
        kernel,
        in_specs=in_specs,
        out_specs=[VMEM] * len(outs),
        out_shape=outs,
        cost_estimate=pl.CostEstimate(flops=flops, bytes_accessed=2**20, transcendentals=0),
        compiler_params=pltpu.CompilerParams(vmem_limit_bytes=8 * 2**20),
        name=name,
    )


def local(query_act, key_act, value_act, filter_taps, skip_gain, out_weight):
    chan = lax.axis_index("chan")
    both = ("seq", "chan")
    send, token = pl.pallas_call(
        pack_kernel,
        out_shape=[
            jax.ShapeDtypeStruct((N_SEQ, 3, 2, 16, LANES), jnp.bfloat16),
            jax.ShapeDtypeStruct((8, LANES), jnp.float32),
        ],
        in_specs=[VMEM] * 4,
        out_specs=[VMEM] * 2,
        name="pack",
    )(query_act, key_act, value_act, filter_taps)
    place = jnp.reshape(chan, (1,)).astype(jnp.int32)
    every = (0, 1, 2, 3)
    ring_w, diag_w, core_w = weight_slices(((2, every), (3, every), (1, every)), 59, out_weight, place, token)
    own_w = weight_slices(tuple((0, (n,)) for n in every), 59, out_weight, place, token)
    own_w = [jnp.reshape(part, (256, 512)) for part in own_w]
    ring_w = lax.ppermute(ring_w, both, ring_y_perm(1, 0))
    diag_w = lax.ppermute(diag_w, both, ring_y_perm(-1, 1))
    core_w = lax.ppermute(core_w, "chan", chan_perm(0, 0, 1))

    gain = lax.dynamic_slice(skip_gain, (16 * lax.axis_index("seq"),), (16,))
    gain = jnp.broadcast_to(gain[:, None], (16, LANES))
    tile = jax.ShapeDtypeStruct((16, LANES), jnp.float32)
    (gain,) = in_vmem(gain_kernel, [VMEM, ANY], [tile], "gain", 0)(gain, own_w[2])
    recv = lax.all_to_all(send, "seq", 0, 0, tiled=True)
    rows = pl.pallas_call(
        conv_kernel,
        out_shape=jax.ShapeDtypeStruct((N_SEQ, 2, 2, 16, LANES), jnp.bfloat16),
        in_specs=[VMEM, VMEM],
        out_specs=ANY,
        scratch_shapes=[pltpu.VMEM((512, LANES), jnp.float32)] * 3
        + [
            pltpu.VMEM((2, 64, LANES), jnp.float32),
            pltpu.VMEM((N_SEQ, 2, 16, LANES), jnp.bfloat16),
            pltpu.SemaphoreType.DMA((2,)),
        ],
        cost_estimate=pl.CostEstimate(flops=2 * 16 * 4096 * 4096, bytes_accessed=0, transcendentals=0),
        compiler_params=pltpu.CompilerParams(vmem_limit_bytes=8 * 2**20),
        name="conv",
    )(recv, gain)
    rows = jnp.reshape(rows, (2 * N_SEQ, 2, 16, LANES))
    rows = lax.all_to_all(rows, both, 0, 0, axis_index_groups=seq_y_groups(), tiled=True)
    rows = jnp.reshape(rows, (N_SEQ, 2, 2, 16, LANES))
    core_rows = lax.ppermute(rows, "chan", chan_perm(0, 0, 1))
    flops = 2 * 256 * 512 * 512
    narrow, wide = jax.ShapeDtypeStruct((256, 512), jnp.bfloat16), jax.ShapeDtypeStruct((256, 512), jnp.float32)
    mine_r, mine = in_vmem(mine_kernel, [SMEM] + [VMEM] * 3, [narrow, wide], "mine", flops)(
        place, own_w[2], ring_w, rows
    )
    core_r, far = in_vmem(far_kernel, [SMEM] + [VMEM] * 4, [narrow] * 2, "far", flops)(
        place, mine, core_w, diag_w, core_rows
    )

    def near(n, after, kind):
        call = in_vmem(functools.partial(near_kernel, n), [VMEM] * 6 + [ANY], [kind], "near", 2 * flops)
        return call(own_w[n], ring_w, core_w, diag_w, mine_r, core_r, after)[0]

    up = near(1, far, narrow)
    down = near(3, up, narrow)
    own = near(0, down, wide)
    far = lax.ppermute(far, "chan", chan_perm(2, 0, 0))
    up = lax.ppermute(up, "chan", chan_perm(1, 0, 0))
    down = lax.ppermute(down, "chan", chan_perm(-1, 0, 0))
    (two,) = in_vmem(two_kernel, [VMEM] * 2, [wide], "two", 0)(own, far)
    out = jax.ShapeDtypeStruct((512, 256), jnp.bfloat16)
    return in_vmem(sum_kernel, [VMEM] * 3, [out], "sum", 0)(two, up, down)[0]


def solution(mesh):
    placed = (
        P("chan", "seq"),
        P("chan", "seq"),
        P("chan", "seq"),
        P("chan", "seq"),
        P("chan"),
        P("chan", None),
    )
    return jax.shard_map(
        local, mesh=mesh, in_specs=placed, out_specs=P("chan", "seq"), check_vma=False
    )
```

```python
import functools

import jax
import jax.numpy as jnp
from jax import lax
from jax.experimental import pallas as pl
from jax.experimental.pallas import tpu as pltpu
from jax.sharding import PartitionSpec as P

N_SEQ, N_X, N_CHAN = 16, 4, 16
LANES = 128
VMEM = pl.BlockSpec(memory_space=pltpu.VMEM)
SMEM = pl.BlockSpec(memory_space=pltpu.SMEM)
ANY = pl.BlockSpec(memory_space=pl.ANY)


def chan_perm(dx, dy, dk):
    return [
        ((x * 2 + y) * 2 + k, ((x + dx) % N_X * 2 + (y ^ dy)) * 2 + (k ^ dk))
        for x in range(N_X)
        for y in range(2)
        for k in range(2)
    ]


def ring_y_perm(step, dk):
    pairs = []
    for y in range(4):
        to = (y + step) % 4
        for z in range(8):
            for x in range(N_X):
                for k in range(2):
                    source = (y // 2 * 8 + z) * N_CHAN + (x * 2 + y % 2) * 2 + k
                    target = (to // 2 * 8 + z) * N_CHAN + (x * 2 + to % 2) * 2 + (k ^ dk)
                    pairs.append((source, target))
    return pairs


def seq_y_groups():
    return [
        [seq * N_CHAN + (x * 2 + y) * 2 + k for seq in range(N_SEQ) for y in range(2)]
        for x in range(N_X)
        for k in range(2)
    ]


def pack_kernel(query_ref, key_ref, value_ref, taps_ref, out_ref, token_ref):
    for dst in range(N_SEQ):
        rows = slice(16 * dst, 16 * dst + 16)
        for half in range(2):
            cols = slice(LANES * half, LANES * half + LANES)
            gated = key_ref[rows, cols].astype(jnp.float32) * value_ref[rows, cols].astype(jnp.float32)
            out_ref[dst, 0, half] = gated.astype(jnp.bfloat16)
            out_ref[dst, 1, half] = taps_ref[rows, cols].astype(jnp.bfloat16)
            out_ref[dst, 2, half] = query_ref[rows, cols]
    token_ref[...] = jnp.zeros_like(token_ref)


def conv_kernel(recv_ref, gain_ref, out_ref, xs, hs, ys, xpad):
    for s in range(N_SEQ):
        for half in range(2):
            rows = slice(32 * s + 16 * half, 32 * s + 16 * half + 16)
            xs[rows, :] = recv_ref[s, 0, half].astype(jnp.float32)
            hs[rows, :] = recv_ref[s, 1, half].astype(jnp.float32)
    for b in range(2):
        xpad[b, 0:32, :] = jnp.zeros((32, LANES), jnp.float32)
    lane = lax.broadcasted_iota(jnp.int32, (8, LANES), 1)
    row = lax.broadcasted_iota(jnp.int32, (8, LANES), 0)
    inside = [lane + row < LANES - 8 * g for g in range(16)]

    def body(p, carry):
        for b in range(2):
            xpad[b, 32:64, :] = xs[pl.ds(2 * p + b, 32, stride=16), :]
        before = [jnp.zeros((8, LANES), jnp.float32)] * 2
        total = jnp.zeros((64, 2 * LANES), jnp.float32)
        for d in range(32):
            shifted = jnp.concatenate([xpad[b, 32 - d : 64 - d, :] for b in range(2)], 0).astype(jnp.bfloat16)
            blocks = []
            for b in range(2):
                taps = jnp.broadcast_to(hs[pl.ds(16 * d + 2 * p + b, 1), :], (8, LANES))
                tiles = [
                    pltpu.roll(jnp.where(inside[g], taps, before[b]), 8 * g, 1, stride=1, stride_axis=0)
                    for g in range(16)
                ]
                before[b] = taps
                blocks.append(jnp.concatenate(tiles, 0).astype(jnp.bfloat16))
            total += jnp.dot(shifted, jnp.concatenate(blocks, 1), preferred_element_type=jnp.float32)
        ys[pl.ds(2 * p, 32, stride=16), :] = total[:32, :LANES]
        ys[pl.ds(2 * p + 1, 32, stride=16), :] = total[32:, LANES:]
        return carry

    lax.fori_loop(0, 8, body, 0, unroll=8)
    for s in range(N_SEQ):
        for half in range(2):
            rows = slice(32 * s + 16 * half, 32 * s + 16 * half + 16)
            total = ys[rows, :] + gain_ref[...] * xs[rows, :]
            gated = (recv_ref[s, 2, half].astype(jnp.float32) * total).astype(jnp.bfloat16)
            out_ref[s, 0, half] = gated
            out_ref[s, 1, half] = gated


def slice_kernel(parts, place_ref, after_ref, weight_ref, *refs):
    outs, held, in_sems, out_sems = refs[: len(parts)], refs[len(parts) : -2], refs[-2], refs[-1]
    loads, stores = [], []
    for number, (other, steps) in enumerate(parts):
        for slot, n in enumerate(steps):
            column = (place_ref[0] // 4 + n) % N_X * 4 + ((place_ref[0] % 4) ^ other)
            source = weight_ref.at[:, pl.ds(pl.multiple_of(column * 512, 512), 512)]
            loads.append((number, pltpu.make_async_copy(source, held[number].at[slot], in_sems.at[number, slot])))
            loads[-1][1].start()
    for number in range(len(parts)):
        for at, load in loads:
            if at == number:
                load.wait()
        stores.append(pltpu.make_async_copy(held[number], outs[number], out_sems.at[number]))
        stores[-1].start()
    for store in stores:
        store.wait()


def weight_slices(parts, limit, weight, place, after):
    shapes = [(len(steps), 256, 512) for other, steps in parts]
    return pl.pallas_call(
        functools.partial(slice_kernel, parts),
        in_specs=[SMEM, ANY, ANY],
        out_specs=[ANY] * len(parts),
        out_shape=[jax.ShapeDtypeStruct(shape, jnp.bfloat16) for shape in shapes],
        scratch_shapes=[pltpu.VMEM(shape, jnp.bfloat16) for shape in shapes]
        + [pltpu.SemaphoreType.DMA((len(parts), N_X)), pltpu.SemaphoreType.DMA((len(parts),))],
        cost_estimate=pl.CostEstimate(flops=0, bytes_accessed=len(parts) * 2**20, transcendentals=0),
        compiler_params=pltpu.CompilerParams(vmem_limit_bytes=limit * 2**20),
        name="weight_slices",
    )(place, after, weight)


def by_position(rows_ref, y):
    halves = [jnp.concatenate([rows_ref[src, y, half] for src in range(N_SEQ)], 0) for half in range(2)]
    return jnp.concatenate([half.astype(jnp.float32).T.astype(jnp.bfloat16) for half in halves], 0)


def product(rows, first, second):
    total = jnp.dot(rows[:, :256], first, preferred_element_type=jnp.float32)
    return total + jnp.dot(rows[:, 256:], second, preferred_element_type=jnp.float32)


def mine_kernel(place_ref, own_w, ring_w, rows_ref, rows_out, out_ref):
    y = place_ref[0] // 2 % 2
    rows_out[:, :256] = by_position(rows_ref, y)
    rows_out[:, 256:] = by_position(rows_ref, 1 - y)
    out_ref[...] = product(rows_out, own_w[...], ring_w[2])


def far_kernel(place_ref, mine, core_w, diag_w, rows_ref, rows_out, first_out, second_out):
    y = place_ref[0] // 2 % 2
    rows_out[:, :256] = by_position(rows_ref, y)
    rows_out[:, 256:] = by_position(rows_ref, 1 - y)
    total = (mine[...] + product(rows_out, core_w[2], diag_w[2])).astype(jnp.bfloat16)
    first_out[...] = total[:LANES, :]
    second_out[...] = total[LANES:, :]


def near_kernel(n, own_w, ring_w, core_w, diag_w, mine_r, core_r, after, first_out, second_out):
    total = product(mine_r, own_w[...], ring_w[n]) + product(core_r, core_w[n], diag_w[n])
    first_out[...] = total[:LANES, :].astype(first_out.dtype)
    second_out[...] = total[LANES:, :].astype(second_out.dtype)


def relay_kernel(near, arrived, out_ref):
    out_ref[...] = (near[...] + arrived[...].astype(jnp.float32)).astype(jnp.bfloat16)


def two_kernel(own_a, own_b, above, below, out_ref):
    out_ref[:LANES, :] = own_a[...] + above[...].astype(jnp.float32)
    out_ref[LANES:, :] = own_b[...] + below[...].astype(jnp.float32)


def sum_kernel(two, below, above, out_ref, held, sems):
    stores = []
    for part in range(4):
        at = slice(LANES * part, LANES * part + LANES)
        held[at, :LANES] = (two[:LANES, at] + below[:, at].astype(jnp.float32)).T.astype(jnp.bfloat16)
        held[at, LANES:] = (two[LANES:, at] + above[:, at].astype(jnp.float32)).T.astype(jnp.bfloat16)
        stores.append(pltpu.make_async_copy(held.at[at], out_ref.at[at], sems.at[part]))
        stores[-1].start()
    for store in stores:
        store.wait()


def gain_kernel(gain_ref, after, out_ref):
    out_ref[...] = gain_ref[...]


def in_vmem(kernel, in_specs, outs, name, flops):
    return pl.pallas_call(
        kernel,
        in_specs=in_specs,
        out_specs=[VMEM] * len(outs),
        out_shape=outs,
        cost_estimate=pl.CostEstimate(flops=flops, bytes_accessed=2**20, transcendentals=0),
        compiler_params=pltpu.CompilerParams(vmem_limit_bytes=8 * 2**20),
        name=name,
    )


def local(query_act, key_act, value_act, filter_taps, skip_gain, out_weight):
    chan = lax.axis_index("chan")
    both = ("seq", "chan")
    send, token = pl.pallas_call(
        pack_kernel,
        out_shape=[
            jax.ShapeDtypeStruct((N_SEQ, 3, 2, 16, LANES), jnp.bfloat16),
            jax.ShapeDtypeStruct((8, LANES), jnp.float32),
        ],
        in_specs=[VMEM] * 4,
        out_specs=[VMEM] * 2,
        name="pack",
    )(query_act, key_act, value_act, filter_taps)
    place = jnp.reshape(chan, (1,)).astype(jnp.int32)
    every = (0, 1, 2, 3)
    ring_w, diag_w, core_w = weight_slices(((2, every), (3, every), (1, every)), 59, out_weight, place, token)
    own_w = weight_slices(tuple((0, (n,)) for n in every), 59, out_weight, place, token)
    own_w = [jnp.reshape(part, (256, 512)) for part in own_w]
    ring_w = lax.ppermute(ring_w, both, ring_y_perm(1, 0))
    diag_w = lax.ppermute(diag_w, both, ring_y_perm(-1, 1))
    core_w = lax.ppermute(core_w, "chan", chan_perm(0, 0, 1))

    gain = lax.dynamic_slice(skip_gain, (16 * lax.axis_index("seq"),), (16,))
    gain = jnp.broadcast_to(gain[:, None], (16, LANES))
    tile = jax.ShapeDtypeStruct((16, LANES), jnp.float32)
    (gain,) = in_vmem(gain_kernel, [VMEM, ANY], [tile], "gain", 0)(gain, own_w[2])
    recv = lax.all_to_all(send, "seq", 0, 0, tiled=True)
    rows = pl.pallas_call(
        conv_kernel,
        out_shape=jax.ShapeDtypeStruct((N_SEQ, 2, 2, 16, LANES), jnp.bfloat16),
        in_specs=[VMEM, VMEM],
        out_specs=VMEM,
        scratch_shapes=[pltpu.VMEM((512, LANES), jnp.float32)] * 3 + [pltpu.VMEM((2, 64, LANES), jnp.float32)],
        cost_estimate=pl.CostEstimate(flops=2 * 16 * 4096 * 4096, bytes_accessed=0, transcendentals=0),
        compiler_params=pltpu.CompilerParams(vmem_limit_bytes=8 * 2**20),
        name="conv",
    )(recv, gain)
    rows = jnp.reshape(rows, (2 * N_SEQ, 2, 16, LANES))
    rows = lax.all_to_all(rows, both, 0, 0, axis_index_groups=seq_y_groups(), tiled=True)
    rows = jnp.reshape(rows, (N_SEQ, 2, 2, 16, LANES))
    core_rows = lax.ppermute(rows, "chan", chan_perm(0, 0, 1))
    flops = 2 * 256 * 512 * 512
    narrow, wide = jax.ShapeDtypeStruct((256, 512), jnp.bfloat16), jax.ShapeDtypeStruct((256, 512), jnp.float32)
    mine_r, mine = in_vmem(mine_kernel, [SMEM] + [VMEM] * 3, [narrow, wide], "mine", flops)(
        place, own_w[2], ring_w, rows
    )
    half = jax.ShapeDtypeStruct((LANES, 512), jnp.bfloat16)
    kept = jax.ShapeDtypeStruct((LANES, 512), jnp.float32)
    core_r, far_a, far_b = in_vmem(far_kernel, [SMEM] + [VMEM] * 4, [narrow, half, half], "far", flops)(
        place, mine, core_w, diag_w, core_rows
    )

    def near(n, after, kinds):
        call = in_vmem(functools.partial(near_kernel, n), [VMEM] * 6 + [ANY], kinds, "near", 2 * flops)
        return call(own_w[n], ring_w, core_w, diag_w, mine_r, core_r, after)

    up_a, up_b = near(1, far_b, [kept, half])
    down_a, down_b = near(3, up_b, [half, kept])
    own_a, own_b = near(0, down_a, [kept, kept])
    upward, downward = chan_perm(1, 0, 0), chan_perm(-1, 0, 0)
    far_a, far_b = lax.ppermute(far_a, "chan", upward), lax.ppermute(far_b, "chan", downward)
    up_b, down_a = lax.ppermute(up_b, "chan", upward), lax.ppermute(down_a, "chan", downward)
    (up_a,) = in_vmem(relay_kernel, [VMEM] * 2, [half], "relay", 0)(up_a, far_a)
    (down_b,) = in_vmem(relay_kernel, [VMEM] * 2, [half], "relay", 0)(down_b, far_b)
    up_a, down_b = lax.ppermute(up_a, "chan", upward), lax.ppermute(down_b, "chan", downward)
    (two,) = in_vmem(two_kernel, [VMEM] * 4, [wide], "two", 0)(own_a, own_b, down_a, up_b)
    out = jax.ShapeDtypeStruct((512, 256), jnp.bfloat16)
    return pl.pallas_call(
        sum_kernel,
        in_specs=[VMEM] * 3,
        out_specs=ANY,
        out_shape=out,
        scratch_shapes=[pltpu.VMEM((512, 256), jnp.bfloat16), pltpu.SemaphoreType.DMA((4,))],
        compiler_params=pltpu.CompilerParams(vmem_limit_bytes=8 * 2**20),
        name="sum",
    )(two, up_a, down_b)


def solution(mesh):
    placed = (
        P("chan", "seq"),
        P("chan", "seq"),
        P("chan", "seq"),
        P("chan", "seq"),
        P("chan"),
        P("chan", None),
    )
    return jax.shard_map(
        local, mesh=mesh, in_specs=placed, out_specs=P("chan", "seq"), check_vma=False
    )
```

```python
import functools

import jax
import jax.numpy as jnp
from jax import lax
from jax.experimental import pallas as pl
from jax.experimental.pallas import tpu as pltpu
from jax.sharding import PartitionSpec as P

N_SEQ, N_X, N_CHAN = 16, 4, 16
LANES = 128
VMEM = pl.BlockSpec(memory_space=pltpu.VMEM)
SMEM = pl.BlockSpec(memory_space=pltpu.SMEM)
ANY = pl.BlockSpec(memory_space=pl.ANY)


def chan_perm(dx, dy, dk):
    return [
        ((x * 2 + y) * 2 + k, ((x + dx) % N_X * 2 + (y ^ dy)) * 2 + (k ^ dk))
        for x in range(N_X)
        for y in range(2)
        for k in range(2)
    ]


def ring_y_perm(step, dk):
    pairs = []
    for y in range(4):
        to = (y + step) % 4
        for z in range(8):
            for x in range(N_X):
                for k in range(2):
                    source = (y // 2 * 8 + z) * N_CHAN + (x * 2 + y % 2) * 2 + k
                    target = (to // 2 * 8 + z) * N_CHAN + (x * 2 + to % 2) * 2 + (k ^ dk)
                    pairs.append((source, target))
    return pairs


def seq_y_groups():
    return [
        [seq * N_CHAN + (x * 2 + y) * 2 + k for seq in range(N_SEQ) for y in range(2)]
        for x in range(N_X)
        for k in range(2)
    ]


def pack_kernel(query_ref, key_ref, value_ref, taps_ref, out_ref, token_ref):
    for dst in range(N_SEQ):
        rows = slice(16 * dst, 16 * dst + 16)
        for half in range(2):
            cols = slice(LANES * half, LANES * half + LANES)
            gated = key_ref[rows, cols].astype(jnp.float32) * value_ref[rows, cols].astype(jnp.float32)
            out_ref[dst, 0, half] = gated.astype(jnp.bfloat16)
            out_ref[dst, 1, half] = taps_ref[rows, cols].astype(jnp.bfloat16)
            out_ref[dst, 2, half] = query_ref[rows, cols]
    token_ref[...] = jnp.zeros_like(token_ref)


def conv_kernel(recv_ref, gain_ref, out_ref, xs, hs, ys, xpad):
    for s in range(N_SEQ):
        for half in range(2):
            rows = slice(32 * s + 16 * half, 32 * s + 16 * half + 16)
            xs[rows, :] = recv_ref[s, 0, half].astype(jnp.float32)
            hs[rows, :] = recv_ref[s, 1, half].astype(jnp.float32)
    for b in range(2):
        xpad[b, 0:32, :] = jnp.zeros((32, LANES), jnp.float32)
    lane = lax.broadcasted_iota(jnp.int32, (8, LANES), 1)
    row = lax.broadcasted_iota(jnp.int32, (8, LANES), 0)
    inside = [lane + row < LANES - 8 * g for g in range(16)]

    def body(p, carry):
        for b in range(2):
            xpad[b, 32:64, :] = xs[pl.ds(2 * p + b, 32, stride=16), :]
        before = [jnp.zeros((8, LANES), jnp.float32)] * 2
        total = jnp.zeros((64, 2 * LANES), jnp.float32)
        for d in range(32):
            shifted = jnp.concatenate([xpad[b, 32 - d : 64 - d, :] for b in range(2)], 0).astype(jnp.bfloat16)
            blocks = []
            for b in range(2):
                taps = jnp.broadcast_to(hs[pl.ds(16 * d + 2 * p + b, 1), :], (8, LANES))
                tiles = [
                    pltpu.roll(jnp.where(inside[g], taps, before[b]), 8 * g, 1, stride=1, stride_axis=0)
                    for g in range(16)
                ]
                before[b] = taps
                blocks.append(jnp.concatenate(tiles, 0).astype(jnp.bfloat16))
            total += jnp.dot(shifted, jnp.concatenate(blocks, 1), preferred_element_type=jnp.float32)
        ys[pl.ds(2 * p, 32, stride=16), :] = total[:32, :LANES]
        ys[pl.ds(2 * p + 1, 32, stride=16), :] = total[32:, LANES:]
        return carry

    lax.fori_loop(0, 8, body, 0, unroll=8)
    for s in range(N_SEQ):
        for half in range(2):
            rows = slice(32 * s + 16 * half, 32 * s + 16 * half + 16)
            total = ys[rows, :] + gain_ref[...] * xs[rows, :]
            gated = (recv_ref[s, 2, half].astype(jnp.float32) * total).astype(jnp.bfloat16)
            out_ref[s, 0, half] = gated
            out_ref[s, 1, half] = gated


def slice_kernel(parts, place_ref, after_ref, weight_ref, *refs):
    outs, held, in_sems, out_sems = refs[: len(parts)], refs[len(parts) : -2], refs[-2], refs[-1]
    loads, stores = [], []
    for number, (other, steps) in enumerate(parts):
        for slot, n in enumerate(steps):
            column = (place_ref[0] // 4 + n) % N_X * 4 + ((place_ref[0] % 4) ^ other)
            source = weight_ref.at[:, pl.ds(pl.multiple_of(column * 512, 512), 512)]
            loads.append((number, pltpu.make_async_copy(source, held[number].at[slot], in_sems.at[number, slot])))
            loads[-1][1].start()
    for number in range(len(parts)):
        for at, load in loads:
            if at == number:
                load.wait()
        stores.append(pltpu.make_async_copy(held[number], outs[number], out_sems.at[number]))
        stores[-1].start()
    for store in stores:
        store.wait()


def weight_slices(parts, limit, weight, place, after):
    shapes = [(len(steps), 256, 512) for other, steps in parts]
    return pl.pallas_call(
        functools.partial(slice_kernel, parts),
        in_specs=[SMEM, ANY, ANY],
        out_specs=[ANY] * len(parts),
        out_shape=[jax.ShapeDtypeStruct(shape, jnp.bfloat16) for shape in shapes],
        scratch_shapes=[pltpu.VMEM(shape, jnp.bfloat16) for shape in shapes]
        + [pltpu.SemaphoreType.DMA((len(parts), N_X)), pltpu.SemaphoreType.DMA((len(parts),))],
        cost_estimate=pl.CostEstimate(flops=0, bytes_accessed=len(parts) * 2**20, transcendentals=0),
        compiler_params=pltpu.CompilerParams(vmem_limit_bytes=limit * 2**20),
        name="weight_slices",
    )(place, after, weight)


def by_position(rows_ref, y):
    halves = [jnp.concatenate([rows_ref[src, y, half] for src in range(N_SEQ)], 0) for half in range(2)]
    return jnp.concatenate([half.astype(jnp.float32).T.astype(jnp.bfloat16) for half in halves], 0)


def product(rows, first, second):
    total = jnp.dot(rows[:, :256], first, preferred_element_type=jnp.float32)
    return total + jnp.dot(rows[:, 256:], second, preferred_element_type=jnp.float32)


def mine_kernel(place_ref, own_w, ring_w, rows_ref, rows_out, out_ref):
    y = place_ref[0] // 2 % 2
    rows_out[:, :256] = by_position(rows_ref, y)
    rows_out[:, 256:] = by_position(rows_ref, 1 - y)
    out_ref[...] = product(rows_out, own_w[...], ring_w[2])


def far_kernel(place_ref, mine, core_w, diag_w, rows_ref, rows_out, first_out, second_out):
    y = place_ref[0] // 2 % 2
    rows_out[:, :256] = by_position(rows_ref, y)
    rows_out[:, 256:] = by_position(rows_ref, 1 - y)
    total = (mine[...] + product(rows_out, core_w[2], diag_w[2])).astype(jnp.bfloat16)
    first_out[...] = total[:LANES, :]
    second_out[...] = total[LANES:, :]


def near_kernel(n, own_w, ring_w, core_w, diag_w, mine_r, core_r, after, first_out, second_out):
    total = product(mine_r, own_w[...], ring_w[n]) + product(core_r, core_w[n], diag_w[n])
    first_out[...] = total[:LANES, :].astype(first_out.dtype)
    second_out[...] = total[LANES:, :].astype(second_out.dtype)


def relay_kernel(near, arrived, out_ref):
    out_ref[...] = (near[...] + arrived[...].astype(jnp.float32)).astype(jnp.bfloat16)


def two_kernel(own_a, own_b, above, below, out_ref):
    out_ref[:LANES, :] = own_a[...] + above[...].astype(jnp.float32)
    out_ref[LANES:, :] = own_b[...] + below[...].astype(jnp.float32)


def sum_kernel(part, two, relayed, *refs):
    out_ref, held, sems = refs[-3:]
    rows = slice(LANES * part, LANES * part + LANES)
    stores = []
    for piece in range(2):
        at = slice(256 * piece, 256 * piece + 256)
        held[at, :] = (two[rows, at] + relayed[:, at].astype(jnp.float32)).T.astype(jnp.bfloat16)
        stores.append(pltpu.make_async_copy(held.at[at], out_ref.at[at, pl.ds(LANES * part, LANES)], sems.at[piece]))
        stores[-1].start()
    for store in stores:
        store.wait()


def write_half(part, two, relayed, *before):
    return pl.pallas_call(
        functools.partial(sum_kernel, part),
        in_specs=[VMEM] * 2 + [ANY] * len(before),
        out_specs=ANY,
        out_shape=jax.ShapeDtypeStruct((512, 256), jnp.bfloat16),
        input_output_aliases={2: 0} if before else {},
        scratch_shapes=[pltpu.VMEM((512, LANES), jnp.bfloat16), pltpu.SemaphoreType.DMA((2,))],
        compiler_params=pltpu.CompilerParams(vmem_limit_bytes=8 * 2**20),
        name="sum",
    )(two, relayed, *before)


def gain_kernel(gain_ref, after, out_ref):
    out_ref[...] = gain_ref[...]


def in_vmem(kernel, in_specs, outs, name, flops):
    return pl.pallas_call(
        kernel,
        in_specs=in_specs,
        out_specs=[VMEM] * len(outs),
        out_shape=outs,
        cost_estimate=pl.CostEstimate(flops=flops, bytes_accessed=2**20, transcendentals=0),
        compiler_params=pltpu.CompilerParams(vmem_limit_bytes=8 * 2**20),
        name=name,
    )


def local(query_act, key_act, value_act, filter_taps, skip_gain, out_weight):
    chan = lax.axis_index("chan")
    both = ("seq", "chan")
    send, token = pl.pallas_call(
        pack_kernel,
        out_shape=[
            jax.ShapeDtypeStruct((N_SEQ, 3, 2, 16, LANES), jnp.bfloat16),
            jax.ShapeDtypeStruct((8, LANES), jnp.float32),
        ],
        in_specs=[VMEM] * 4,
        out_specs=[VMEM] * 2,
        name="pack",
    )(query_act, key_act, value_act, filter_taps)
    place = jnp.reshape(chan, (1,)).astype(jnp.int32)
    every = (0, 1, 2, 3)
    ring_w, diag_w, core_w = weight_slices(((2, every), (3, every), (1, every)), 59, out_weight, place, token)
    own_w = weight_slices(tuple((0, (n,)) for n in every), 59, out_weight, place, token)
    own_w = [jnp.reshape(part, (256, 512)) for part in own_w]
    ring_w = lax.ppermute(ring_w, both, ring_y_perm(1, 0))
    diag_w = lax.ppermute(diag_w, both, ring_y_perm(-1, 1))
    core_w = lax.ppermute(core_w, "chan", chan_perm(0, 0, 1))

    gain = lax.dynamic_slice(skip_gain, (16 * lax.axis_index("seq"),), (16,))
    gain = jnp.broadcast_to(gain[:, None], (16, LANES))
    tile = jax.ShapeDtypeStruct((16, LANES), jnp.float32)
    (gain,) = in_vmem(gain_kernel, [VMEM, ANY], [tile], "gain", 0)(gain, own_w[2])
    recv = lax.all_to_all(send, "seq", 0, 0, tiled=True)
    rows = pl.pallas_call(
        conv_kernel,
        out_shape=jax.ShapeDtypeStruct((N_SEQ, 2, 2, 16, LANES), jnp.bfloat16),
        in_specs=[VMEM, VMEM],
        out_specs=VMEM,
        scratch_shapes=[pltpu.VMEM((512, LANES), jnp.float32)] * 3 + [pltpu.VMEM((2, 64, LANES), jnp.float32)],
        cost_estimate=pl.CostEstimate(flops=2 * 16 * 4096 * 4096, bytes_accessed=0, transcendentals=0),
        compiler_params=pltpu.CompilerParams(vmem_limit_bytes=8 * 2**20),
        name="conv",
    )(recv, gain)
    rows = jnp.reshape(rows, (2 * N_SEQ, 2, 16, LANES))
    rows = lax.all_to_all(rows, both, 0, 0, axis_index_groups=seq_y_groups(), tiled=True)
    rows = jnp.reshape(rows, (N_SEQ, 2, 2, 16, LANES))
    core_rows = lax.ppermute(rows, "chan", chan_perm(0, 0, 1))
    flops = 2 * 256 * 512 * 512
    narrow, wide = jax.ShapeDtypeStruct((256, 512), jnp.bfloat16), jax.ShapeDtypeStruct((256, 512), jnp.float32)
    mine_r, mine = in_vmem(mine_kernel, [SMEM] + [VMEM] * 3, [narrow, wide], "mine", flops)(
        place, own_w[2], ring_w, rows
    )
    half = jax.ShapeDtypeStruct((LANES, 512), jnp.bfloat16)
    kept = jax.ShapeDtypeStruct((LANES, 512), jnp.float32)
    core_r, far_a, far_b = in_vmem(far_kernel, [SMEM] + [VMEM] * 4, [narrow, half, half], "far", flops)(
        place, mine, core_w, diag_w, core_rows
    )

    def near(n, after, kinds):
        call = in_vmem(functools.partial(near_kernel, n), [VMEM] * 6 + [ANY], kinds, "near", 2 * flops)
        return call(own_w[n], ring_w, core_w, diag_w, mine_r, core_r, after)

    up_a, up_b = near(1, far_b, [kept, half])
    down_a, down_b = near(3, up_b, [half, kept])
    own_a, own_b = near(0, down_a, [kept, kept])
    upward, downward = chan_perm(1, 0, 0), chan_perm(-1, 0, 0)
    far_a, far_b = lax.ppermute(far_a, "chan", upward), lax.ppermute(far_b, "chan", downward)
    up_b, down_a = lax.ppermute(up_b, "chan", upward), lax.ppermute(down_a, "chan", downward)
    (up_a,) = in_vmem(relay_kernel, [VMEM] * 2, [half], "relay", 0)(up_a, far_a)
    (down_b,) = in_vmem(relay_kernel, [VMEM] * 2, [half], "relay", 0)(down_b, far_b)
    up_a, down_b = lax.ppermute(up_a, "chan", upward), lax.ppermute(down_b, "chan", downward)
    (two,) = in_vmem(two_kernel, [VMEM] * 4, [wide], "two", 0)(own_a, own_b, down_a, up_b)
    return write_half(1, two, down_b, write_half(0, two, up_a))


def solution(mesh):
    placed = (
        P("chan", "seq"),
        P("chan", "seq"),
        P("chan", "seq"),
        P("chan", "seq"),
        P("chan"),
        P("chan", None),
    )
    return jax.shard_map(
        local, mesh=mesh, in_specs=placed, out_specs=P("chan", "seq"), check_vma=False
    )
```
